32 devices in a mesh: circ: 8 (over z, core), axial: 4 (over y, x).
Axes of the slice: x: 2, y: 2, z: 4, core: 2. Of those that a mesh axis runs over, the one named last changes fastest.
Arguments:
- interior_inv: bfloat16 [8, 4, 8, 512, 512], P('circ', 'axial'), as said below
- coupling: bfloat16 [8, 4, 8, 512, 640], P('circ', 'axial'), may hold values from -0.25 to 0.25
- boundary_diag: bfloat16 [8, 4, 8, 5, 128, 128], P('circ', 'axial'), may hold values from -3 to 3
- directions: int32 [8, 4, 8, 5], P('circ', 'axial'), may hold values from 0 to 4, as said below
- slot_ids: int32 [8, 4, 8, 5], P('circ', 'axial'), may hold values from 0 to 7, as said below
- live_blocks: int32 [8, 4, 8], P('circ', 'axial'), may hold values from 1 to 5, as said below
- weights: int32 [8, 4, 8, 5], P('circ', 'axial'), may hold values from 1 to 4
Outputs:
- averaged: float32 [8, 4, 8, 128, 128], P('circ', 'axial')
- deviation: bfloat16 [8, 4, 8, 5, 128, 128], P('circ', 'axial')
The draws below stay inside these ranges and needn't reach their ends.
Inputs may be any that keep to these rules, and one draw needn't show every extreme that they name: `directions`: 0 to 4; never 3 on the last device row along axial, never 4 on the first. `slot_ids`: the slot 7 is named on every device. `live_blocks`: the first subdomain of the first device has all 5 blocks live. `interior_inv`: symmetric.
All inputs are finite; a program needn't handle non-finite values.
Results may differ from the reference program's by a relative error of at most 0.007.
Values may be sent and summed in bfloat16 or wider, within the bound.
No kernel may reach another device: no remote copies, remote signals or barrier semaphores. Data moves between devices by JAX's collectives and lax.ppermute only.
A program may use at most 128 MiB of HBM per device.

```python
import jax
import jax.numpy as jnp
from jax import lax

S = 8
NI = 512
NBLK = 5
BS = 128
OWN = 8
NB = 640
CYCLES = 8
LAYERS = 4


def draw_interior_inv(key, part):
    key = jax.random.fold_in(key, 11)
    shape = (CYCLES, LAYERS, S, NI, NI)
    first, second = jax.random.split(key)
    noise = jax.random.normal(first, shape, jnp.float32)
    diag = jax.random.uniform(second, shape[:-1], jnp.float32, 0.5, 1.5)
    sym = (noise + jnp.swapaxes(noise, -1, -2)) * (0.35 / NI ** 0.5)
    eye = jnp.eye(NI, dtype=jnp.float32)
    return (sym + eye * diag[..., None]).astype(jnp.bfloat16)


def draw_directions(key, part):
    key = jax.random.fold_in(key, 23)
    codes = jax.random.randint(key, (CYCLES, LAYERS, S, NBLK), 0, 5)
    layer = jnp.arange(LAYERS)[None, :, None, None]
    codes = jnp.where((layer == 0) & (codes == 4), 3, codes)
    codes = jnp.where((layer == LAYERS - 1) & (codes == 3), 4, codes)
    return codes.astype(jnp.int32)


def draw_slot_ids(key, part):
    key = jax.random.fold_in(key, 37)
    slots = jax.random.randint(key, (CYCLES, LAYERS, S, NBLK), 0, OWN)
    return slots.at[:, :, 0, 0].set(OWN - 1).astype(jnp.int32)


def draw_live_blocks(key, part):
    key = jax.random.fold_in(key, 41)
    counts = jax.random.randint(key, (CYCLES, LAYERS, S), 1, NBLK + 1)
    return counts.at[0, 0, 0].set(NBLK).astype(jnp.int32)


def with_ends(entries, stream_key, smallest, top_value):
    longest = entries.shape.index(max(entries.shape))
    spots = []
    for shift in (0, 1):
        where = [jax.random.randint(jax.random.fold_in(stream_key, axis), (), 0, length) for axis, length in enumerate(entries.shape)]
        where[longest] = (where[longest] + shift) % entries.shape[longest]
        spots.append(tuple(where))
    return entries.at[spots[0]].set(smallest).at[spots[1]].set(top_value)


def block_levels(own_key, dims, pieces, low, largest):
    def one(dim, blocks):
        draws = jax.random.uniform(jax.random.fold_in(jax.random.fold_in(own_key, 6), dim), (blocks,), jnp.float32, low / len(pieces), largest / len(pieces))
        return jnp.repeat(jnp.exp(draws), dims[dim] // blocks).reshape((-1,) + (1,) * (len(dims) - dim - 1))

    factor_of = one(*pieces[0])
    for cut in pieces[1:]:
        factor_of = factor_of * one(*cut)
    return factor_of


def bell_draw(rng, extent, width, limit, cuts=(), kind=jnp.bfloat16):
    factor_of = block_levels(rng, extent, cuts, -0.22, 0.18) if cuts else 1.0
    result = jax.random.normal(rng, extent, jnp.float32) * width * factor_of
    return jnp.minimum(jnp.maximum(result, -limit), limit).astype(kind)


def setup_inputs(seed: int = 0) -> dict:
    splits = jax.random.split(jax.random.key(seed), 8)
    interior_inv = draw_interior_inv(jax.random.fold_in(splits[7], 71), 0)
    coupling = bell_draw(splits[1], (CYCLES, LAYERS, S, NI, NB), NI ** -0.5, 0.25, ((0, 8), (1, 4)))
    boundary_diag = bell_draw(splits[2], (CYCLES, LAYERS, S, NBLK, BS, BS), 0.5, 3.0, ((0, 8), (1, 4)))
    directions = draw_directions(jax.random.fold_in(splits[7], 71), 0)
    slot_ids = draw_slot_ids(jax.random.fold_in(splits[7], 71), 0)
    live_blocks = draw_live_blocks(jax.random.fold_in(splits[7], 71), 0)
    weights = with_ends(jax.random.randint(splits[6], (CYCLES, LAYERS, S, NBLK), 1, 5), jax.random.fold_in(splits[6], 1), 1, 4).astype(jnp.int32)
    return {"interior_inv": interior_inv, "coupling": coupling, "boundary_diag": boundary_diag, "directions": directions, "slot_ids": slot_ids, "live_blocks": live_blocks, "weights": weights}


def schur_cycle(packed):
    interior_inv, coupling, boundary_diag = packed
    solved = jnp.einsum('lsij,lsjk->lsik', interior_inv.astype(jnp.float32), coupling.astype(jnp.float32)).astype(jnp.bfloat16)
    solved = lax.optimization_barrier(solved).astype(jnp.float32)
    layers, subs = coupling.shape[0], coupling.shape[1]
    left = coupling.astype(jnp.float32).reshape(layers, subs, NI, NBLK, BS)
    right = solved.reshape(layers, subs, NI, NBLK, BS)
    trailing = jnp.einsum('lsinx,lsiny->lsnxy', left, right)
    return (boundary_diag.astype(jnp.float32) - trailing).astype(jnp.bfloat16)


def reference(interior_inv, coupling, boundary_diag, directions, slot_ids, live_blocks, weights):
    schur = lax.map(schur_cycle, (interior_inv, coupling, boundary_diag))
    schur_wide = schur.astype(jnp.float32)
    live_mask = jnp.arange(NBLK)[None, None, None, :] < live_blocks[..., None]
    onehot = (slot_ids[..., None] == jnp.arange(OWN)[None, None, None, None, :]).astype(jnp.float32)
    offsets = ((0, 0), (1, 0), (-1, 0), (0, 1), (0, -1))
    numerator = jnp.zeros((CYCLES, LAYERS, OWN, BS, BS), jnp.float32)
    denominator = jnp.zeros((CYCLES, LAYERS, OWN), jnp.float32)
    for code in range(5):
        cycle_off, layer_off = offsets[code]
        chosen = (live_mask & (directions == code)).astype(jnp.float32) * weights.astype(jnp.float32)
        routing = onehot * chosen[..., None]
        contrib = jnp.einsum('rlsno,rlsnxy->rloxy', routing, schur_wide)
        weight_sum = jnp.sum(routing, axis=(2, 3))
        numerator = numerator + jnp.roll(jnp.roll(contrib, cycle_off, 0), layer_off, 1)
        denominator = denominator + jnp.roll(jnp.roll(weight_sum, cycle_off, 0), layer_off, 1)
    averaged = numerator / jnp.maximum(denominator, 1.0)[..., None, None]
    fetched = jnp.zeros_like(schur_wide)
    for code in range(5):
        cycle_off, layer_off = offsets[code]
        owner_avg = jnp.roll(jnp.roll(averaged, -cycle_off, 0), -layer_off, 1)
        select = onehot * (live_mask & (directions == code)).astype(jnp.float32)[..., None]
        fetched = fetched + jnp.einsum('rlsno,rloxy->rlsnxy', select, owner_avg, precision=lax.Precision.HIGHEST)
    deviation = jnp.where(live_mask[..., None, None], schur_wide - fetched, 0.0).astype(jnp.bfloat16)
    return averaged, deviation
```

```python
import functools

import jax
import jax.numpy as jnp
from jax import lax
from jax.experimental import pallas as pl
from jax.experimental.pallas import tpu as pltpu
from jax.sharding import PartitionSpec as P

PAD = 16


def near_pairs(count):
    return [(i, i ^ 1) for i in range(count)]


def far_pairs(count, periodic):
    pairs = []
    for i in range(count):
        j = i + 1 if i % 2 else i - 1
        if periodic:
            pairs.append((i, j % count))
        elif 0 <= j < count:
            pairs.append((i, j))
    return pairs


def swap_all(to_near_c, to_far_c, to_near_a, to_far_a):
    circ, axial = lax.axis_size("circ"), lax.axis_size("axial")
    near_a = lax.ppermute(to_near_a, "axial", near_pairs(axial))
    far_c = lax.ppermute(to_far_c, "circ", far_pairs(circ, True))
    far_a = lax.ppermute(to_far_a, "axial", far_pairs(axial, False))
    near_c = lax.ppermute(to_near_c, "circ", near_pairs(circ))
    return near_c, far_c, near_a, far_a


def buffer_of(code):
    odd_c = lax.rem(lax.axis_index("circ"), 2)
    odd_a = lax.rem(lax.axis_index("axial"), 2)
    circ = jnp.where(odd_c == 0, code, 3 - code)
    axial = jnp.where(odd_a == 0, code, 7 - code)
    return jnp.where(code == 0, 0, jnp.where(code <= 2, circ, axial))


def schur_kernel(
    dirs, slots, live, weights, inv, coup, diag,
    schur, own, own_cnt, s1, s2, s3, s4,
    inv_v, coup_v, diag_v, acc, cnt, sems,
):
    subs, nblk, bs = diag.shape[0], diag.shape[1], diag.shape[2]
    own_slots = own.shape[0] // bs

    def loads(sub):
        pairs = ((coup, coup_v), (inv, inv_v), (diag, diag_v))
        return [
            pltpu.make_async_copy(a.at[sub], b.at[sub], sems.at[j, sub])
            for j, (a, b) in enumerate(pairs)
        ]

    for sub in range(subs):
        for copy in loads(sub):
            copy.start()
    acc[...] = jnp.zeros_like(acc)
    cnt[...] = jnp.zeros_like(cnt)

    def step(sub, carry):
        for copy in loads(sub):
            copy.wait()
        c = coup_v[sub]
        st = jnp.dot(c.T, inv_v[sub], preferred_element_type=jnp.float32).astype(jnp.bfloat16)
        for k in range(nblk):
            cols = slice(k * bs, (k + 1) * bs)
            trail = jnp.dot(st[cols], c[:, cols], preferred_element_type=jnp.float32)
            block = (diag_v[sub, k].astype(jnp.float32) - trail).astype(jnp.bfloat16)
            schur[sub, k] = block
            w = jnp.where(k < live[0, sub], weights[k, 0, sub], 0).astype(jnp.float32)
            buf, slot = buffer_of(dirs[k, 0, sub]), slots[k, 0, sub]
            acc[buf * own_slots + slot] += w * block.astype(jnp.float32)
            cnt[buf, pl.ds(slot, 1), :] += jnp.full((1, bs), w, jnp.float32)
        return carry

    lax.fori_loop(0, subs, step, 0)
    for o in range(own_slots):
        own[o * bs:(o + 1) * bs] = acc[o]
    own_cnt[...] = cnt[0]
    for b, out in enumerate((s1, s2, s3, s4), 1):
        for o in range(own_slots):
            out[o * bs:(o + 1) * bs] = acc[b * own_slots + o].astype(jnp.bfloat16)
        out[own_slots * bs:] = cnt[b].astype(jnp.bfloat16)


def average_kernel(own, own_cnt, r1, r2, r3, r4, avg, avg_short):
    bs = own.shape[1]
    own_slots = own.shape[0] // bs
    parts = (r1, r2, r3, r4)
    count = own_cnt[...]
    for r in parts:
        count = count + r[own_slots * bs:].astype(jnp.float32)
    scale = 1.0 / jnp.maximum(count, 1.0)
    for o in range(own_slots):
        rows = slice(o * bs, (o + 1) * bs)
        total = own[rows]
        for r in parts:
            total = total + r[rows].astype(jnp.float32)
        mean = total * scale[o:o + 1]
        avg[rows] = mean
        avg_short[rows] = mean.astype(jnp.bfloat16)


def deviation_kernel(dirs, slots, live, schur, avg, r1, r2, r3, r4, dev, table, stage, sems):
    subs, nblk, bs = schur.shape[0], schur.shape[1], schur.shape[2]
    own_slots = avg.shape[0] // bs
    for b, r in enumerate((avg, r1, r2, r3, r4)):
        for o in range(own_slots):
            table[b * own_slots + o] = r[o * bs:(o + 1) * bs]
    stores = []
    for s in range(subs):
        for k in range(nblk):
            at = buffer_of(dirs[k, 0, s]) * own_slots + slots[k, 0, s]
            diff = schur[s, k].astype(jnp.float32) - table[at].astype(jnp.float32)
            stage[s, k] = jnp.where(k < live[0, s], diff, 0.0).astype(jnp.bfloat16)
        stores.append(pltpu.make_async_copy(stage.at[s], dev.at[s], sems.at[s]))
        stores[-1].start()
    for copy in stores:
        copy.wait()


def body(interior_inv, coupling, boundary_diag, directions, slot_ids, live_blocks, weights):
    inv, coup, diag = interior_inv[0, 0], coupling[0, 0], boundary_diag[0, 0]
    subs, ni, nb = coup.shape
    nblk, bs = diag.shape[1], diag.shape[2]
    own_slots = 8
    by_block = lambda x: jnp.transpose(x[0], (2, 0, 1))
    dirs, slots, wts = by_block(directions), by_block(slot_ids), by_block(weights)
    live = live_blocks[0]
    f32, bf16 = jnp.float32, jnp.bfloat16
    rows = own_slots * bs
    smem = pl.BlockSpec(memory_space=pltpu.SMEM)
    vmem = pl.BlockSpec(memory_space=pltpu.VMEM)
    hbm = pl.BlockSpec(memory_space=pltpu.HBM)
    sent = jax.ShapeDtypeStruct((rows + PAD, bs), bf16)
    schur, own, own_cnt, s1, s2, s3, s4 = pl.pallas_call(
        schur_kernel,
        in_specs=[smem] * 4 + [hbm] * 3,
        out_specs=[vmem] * 7,
        out_shape=[
            jax.ShapeDtypeStruct((subs, nblk, bs, bs), bf16),
            jax.ShapeDtypeStruct((rows, bs), f32),
            jax.ShapeDtypeStruct((PAD, bs), f32),
        ] + [sent] * 4,
        scratch_shapes=[
            pltpu.VMEM(inv.shape, bf16),
            pltpu.VMEM(coup.shape, bf16),
            pltpu.VMEM(diag.shape, bf16),
            pltpu.VMEM((5 * own_slots, bs, bs), f32),
            pltpu.VMEM((5, PAD, bs), f32),
            pltpu.SemaphoreType.DMA((3, subs)),
        ],
        compiler_params=pltpu.CompilerParams(vmem_limit_bytes=56 * 2**20),
        name="schur_and_sums",
    )(dirs, slots, live, wts, inv, coup, diag)
    r1, r2, r3, r4 = swap_all(s1, s2, s3, s4)
    avg, avg_short = pl.pallas_call(
        average_kernel,
        in_specs=[vmem] * 6,
        out_specs=[vmem] * 2,
        out_shape=[
            jax.ShapeDtypeStruct((rows, bs), f32),
            jax.ShapeDtypeStruct((rows, bs), bf16),
        ],
        compiler_params=pltpu.CompilerParams(vmem_limit_bytes=16 * 2**20),
        name="average",
    )(own, own_cnt, r1, r2, r3, r4)
    n1, n2, n3, n4 = swap_all(avg_short, avg_short, avg_short, avg_short)
    dev = pl.pallas_call(
        deviation_kernel,
        in_specs=[smem] * 3 + [vmem] * 6,
        out_specs=hbm,
        out_shape=jax.ShapeDtypeStruct((subs, nblk, bs, bs), bf16),
        scratch_shapes=[
            pltpu.VMEM((5 * own_slots, bs, bs), bf16),
            pltpu.VMEM((subs, nblk, bs, bs), bf16),
            pltpu.SemaphoreType.DMA((subs,)),
        ],
        compiler_params=pltpu.CompilerParams(vmem_limit_bytes=16 * 2**20),
        name="deviation",
    )(dirs, slots, live, schur, avg_short, n1, n2, n3, n4)
    return avg.reshape(1, 1, own_slots, bs, bs), dev[None, None]


def solution(mesh):
    return jax.shard_map(
        body,
        mesh=mesh,
        in_specs=(
            P("circ", "axial", None, None, None),
            P("circ", "axial", None, None, None),
            P("circ", "axial", None, None, None, None),
            P("circ", "axial", None, None),
            P("circ", "axial", None, None),
            P("circ", "axial", None),
            P("circ", "axial", None, None),
        ),
        out_specs=(
            P("circ", "axial", None, None, None),
            P("circ", "axial", None, None, None, None),
        ),
        check_vma=False,
    )
```

```python
import functools

import jax
import jax.numpy as jnp
from jax import lax
from jax.experimental import pallas as pl
from jax.experimental.pallas import tpu as pltpu
from jax.sharding import PartitionSpec as P

PAD = 16
SUMS_ORDER = ("near_a", "far_c", "far_a", "near_c")
MEANS_ORDER = ("far_a", "far_c", "near_c", "near_a")


def near_pairs(count):
    return [(i, i ^ 1) for i in range(count)]


def far_pairs(count, periodic):
    pairs = []
    for i in range(count):
        j = i + 1 if i % 2 else i - 1
        if periodic:
            pairs.append((i, j % count))
        elif 0 <= j < count:
            pairs.append((i, j))
    return pairs


NAMES = ("near_c", "far_c", "near_a", "far_a")


def swap_all(sent, order):
    circ, axial = lax.axis_size("circ"), lax.axis_size("axial")
    routes = {
        "near_c": ("circ", near_pairs(circ)),
        "far_c": ("circ", far_pairs(circ, True)),
        "near_a": ("axial", near_pairs(axial)),
        "far_a": ("axial", far_pairs(axial, False)),
    }
    return [lax.ppermute(sent[name], *routes[name]) for name in order]


def buffer_of(code):
    odd_c = lax.rem(lax.axis_index("circ"), 2)
    odd_a = lax.rem(lax.axis_index("axial"), 2)
    circ = jnp.where(odd_c == 0, code, 3 - code)
    axial = jnp.where(odd_a == 0, code, 7 - code)
    return jnp.where(code == 0, 0, jnp.where(code <= 2, circ, axial))


def schur_kernel(
    dirs, slots, live, weights, inv, coup, diag,
    schur, own, own_cnt, s1, s2, s3, s4,
    inv_v, coup_v, diag_v, acc, cnt, sems,
):
    subs, nblk, bs = diag.shape[0], diag.shape[1], diag.shape[2]
    own_slots = own.shape[0] // bs

    def loads(sub):
        pairs = ((coup, coup_v), (inv, inv_v), (diag, diag_v))
        return [
            pltpu.make_async_copy(a.at[sub], b.at[sub], sems.at[j, sub])
            for j, (a, b) in enumerate(pairs)
        ]

    for sub in range(subs):
        for copy in loads(sub):
            copy.start()
    acc[...] = jnp.zeros_like(acc)
    cnt[...] = jnp.zeros_like(cnt)

    def step(sub, carry):
        for copy in loads(sub):
            copy.wait()
        c = coup_v[sub]
        st = jnp.dot(c.T, inv_v[sub], preferred_element_type=jnp.float32).astype(jnp.bfloat16)
        for k in range(nblk):
            cols = slice(k * bs, (k + 1) * bs)
            trail = jnp.dot(st[cols], c[:, cols], preferred_element_type=jnp.float32)
            block = (diag_v[sub, k].astype(jnp.float32) - trail).astype(jnp.bfloat16)
            schur[sub, k] = block
            w = jnp.where(k < live[0, sub], weights[k, 0, sub], 0).astype(jnp.float32)
            buf, slot = buffer_of(dirs[k, 0, sub]), slots[k, 0, sub]
            acc[buf * own_slots + slot] += w * block.astype(jnp.float32)
            cnt[buf, pl.ds(slot, 1), :] += jnp.full((1, bs), w, jnp.float32)
        return carry

    lax.fori_loop(0, subs, step, 0)
    for o in range(own_slots):
        own[o * bs:(o + 1) * bs] = acc[o]
    own_cnt[...] = cnt[0]
    for b, out in enumerate((s1, s2, s3, s4), 1):
        for o in range(own_slots):
            out[o * bs:(o + 1) * bs] = acc[b * own_slots + o].astype(jnp.bfloat16)
        out[own_slots * bs:] = cnt[b].astype(jnp.bfloat16)


def average_kernel(own, own_cnt, r1, r2, r3, r4, avg, avg_short):
    bs = own.shape[1]
    own_slots = own.shape[0] // bs
    parts = (r1, r2, r3, r4)
    count = own_cnt[...]
    for r in parts:
        count = count + r[own_slots * bs:].astype(jnp.float32)
    scale = 1.0 / jnp.maximum(count, 1.0)
    for o in range(own_slots):
        rows = slice(o * bs, (o + 1) * bs)
        total = own[rows]
        for r in parts:
            total = total + r[rows].astype(jnp.float32)
        mean = total * scale[o:o + 1]
        avg[rows] = mean
        avg_short[rows] = mean.astype(jnp.bfloat16)


def deviation_kernel(
    order, dirs, slots, live, schur, avg, r1, r2, r3, r4, dev, table, stage, sems
):
    subs, nblk, bs = schur.shape[0], schur.shape[1], schur.shape[2]
    own_slots = avg.shape[0] // bs
    places = [0] + [1 + NAMES.index(name) for name in order]
    for b, r in zip(places, (avg, r1, r2, r3, r4)):
        for o in range(own_slots):
            table[b * own_slots + o] = r[o * bs:(o + 1) * bs]
    stores = []
    for s in range(subs):
        for k in range(nblk):
            at = buffer_of(dirs[k, 0, s]) * own_slots + slots[k, 0, s]
            diff = schur[s, k].astype(jnp.float32) - table[at].astype(jnp.float32)
            stage[s, k] = jnp.where(k < live[0, s], diff, 0.0).astype(jnp.bfloat16)
        stores.append(pltpu.make_async_copy(stage.at[s], dev.at[s], sems.at[s]))
        stores[-1].start()
    for copy in stores:
        copy.wait()


def body(interior_inv, coupling, boundary_diag, directions, slot_ids, live_blocks, weights):
    inv, coup, diag = interior_inv[0, 0], coupling[0, 0], boundary_diag[0, 0]
    subs, ni, nb = coup.shape
    nblk, bs = diag.shape[1], diag.shape[2]
    own_slots = 8
    by_block = lambda x: jnp.transpose(x[0], (2, 0, 1))
    in_hbm = lambda x: pltpu.with_memory_space_constraint(x, pltpu.HBM)
    dirs, slots, wts = (in_hbm(by_block(x)) for x in (directions, slot_ids, weights))
    live = in_hbm(live_blocks[0])
    f32, bf16 = jnp.float32, jnp.bfloat16
    rows = own_slots * bs
    smem = pl.BlockSpec(memory_space=pltpu.SMEM)
    vmem = pl.BlockSpec(memory_space=pltpu.VMEM)
    hbm = pl.BlockSpec(memory_space=pltpu.HBM)
    schur, own, own_cnt, s1, s2, s3, s4 = pl.pallas_call(
        schur_kernel,
        in_specs=[smem] * 4 + [hbm] * 3,
        out_specs=[vmem] * 7,
        out_shape=[
            pltpu.VMEM((subs, nblk, bs, bs), bf16),
            pltpu.VMEM((rows, bs), f32),
            pltpu.VMEM((PAD, bs), f32),
        ] + [pltpu.VMEM((rows + PAD, bs), bf16)] * 4,
        scratch_shapes=[
            pltpu.VMEM(inv.shape, bf16),
            pltpu.VMEM(coup.shape, bf16),
            pltpu.VMEM(diag.shape, bf16),
            pltpu.VMEM((5 * own_slots, bs, bs), f32),
            pltpu.VMEM((5, PAD, bs), f32),
            pltpu.SemaphoreType.DMA((3, subs)),
        ],
        compiler_params=pltpu.CompilerParams(vmem_limit_bytes=56 * 2**20),
        name="schur_and_sums",
    )(dirs, slots, live, wts, in_hbm(inv), in_hbm(coup), in_hbm(diag))
    received = swap_all(dict(zip(NAMES, (s1, s2, s3, s4))), SUMS_ORDER)
    avg, avg_short = pl.pallas_call(
        average_kernel,
        in_specs=[vmem] * 6,
        out_specs=[vmem] * 2,
        out_shape=[
            jax.ShapeDtypeStruct((rows, bs), f32),
            jax.ShapeDtypeStruct((rows, bs), bf16),
        ],
        compiler_params=pltpu.CompilerParams(vmem_limit_bytes=16 * 2**20),
        name="average",
    )(own, own_cnt, *received)
    fetched = swap_all(dict.fromkeys(NAMES, avg_short), MEANS_ORDER)
    dev = pl.pallas_call(
        functools.partial(deviation_kernel, MEANS_ORDER),
        in_specs=[smem] * 3 + [vmem] * 6,
        out_specs=hbm,
        out_shape=jax.ShapeDtypeStruct((subs, nblk, bs, bs), bf16),
        scratch_shapes=[
            pltpu.VMEM((5 * own_slots, bs, bs), bf16),
            pltpu.VMEM((subs, nblk, bs, bs), bf16),
            pltpu.SemaphoreType.DMA((subs,)),
        ],
        compiler_params=pltpu.CompilerParams(vmem_limit_bytes=16 * 2**20),
        name="deviation",
    )(dirs, slots, live, schur, avg_short, *fetched)
    return avg.reshape(1, 1, own_slots, bs, bs), dev[None, None]


def solution(mesh):
    return jax.shard_map(
        body,
        mesh=mesh,
        in_specs=(
            P("circ", "axial", None, None, None),
            P("circ", "axial", None, None, None),
            P("circ", "axial", None, None, None, None),
            P("circ", "axial", None, None),
            P("circ", "axial", None, None),
            P("circ", "axial", None),
            P("circ", "axial", None, None),
        ),
        out_specs=(
            P("circ", "axial", None, None, None),
            P("circ", "axial", None, None, None, None),
        ),
        check_vma=False,
    )
```

```python
import functools

import jax
import jax.numpy as jnp
from jax import lax
from jax.experimental import pallas as pl
from jax.experimental.pallas import tpu as pltpu
from jax.sharding import PartitionSpec as P

PAD = 16
SUMS_ORDER = ("near_a", "far_c", "far_a", "near_c")
MEANS_ORDER = ("far_a", "far_c", "near_c", "near_a")


def near_pairs(count):
    return [(i, i ^ 1) for i in range(count)]


def far_pairs(count, periodic):
    pairs = []
    for i in range(count):
        j = i + 1 if i % 2 else i - 1
        if periodic:
            pairs.append((i, j % count))
        elif 0 <= j < count:
            pairs.append((i, j))
    return pairs


NAMES = ("near_c", "far_c", "near_a", "far_a")


def swap_all(sent, order):
    circ, axial = lax.axis_size("circ"), lax.axis_size("axial")
    routes = {
        "near_c": ("circ", near_pairs(circ)),
        "far_c": ("circ", far_pairs(circ, True)),
        "near_a": ("axial", near_pairs(axial)),
        "far_a": ("axial", far_pairs(axial, False)),
    }
    diagonal = []
    for row in range(circ):
        for i, j in far_pairs(axial, False):
            diagonal.append((row * axial + i, row * axial + j))
        for i in (0, axial - 1):
            diagonal.append((row * axial + i, (row ^ 1) * axial + i))
    routes["far_a"] = (("circ", "axial"), diagonal)
    return [lax.ppermute(sent[name], *routes[name]) for name in order]


def buffer_of(code):
    odd_c = lax.rem(lax.axis_index("circ"), 2)
    odd_a = lax.rem(lax.axis_index("axial"), 2)
    circ = jnp.where(odd_c == 0, code, 3 - code)
    axial = jnp.where(odd_a == 0, code, 7 - code)
    return jnp.where(code == 0, 0, jnp.where(code <= 2, circ, axial))


def load_tables(sources, tables, sems):
    copies = [
        pltpu.make_async_copy(a, b, sems.at[j]) for j, (a, b) in enumerate(zip(sources, tables))
    ]
    for copy in copies:
        copy.start()
    return copies


def schur_kernel(
    dirs_h, slots_h, live_h, weights_h, inv, coup, diag,
    schur, own, own_cnt, s1, s2, s3, s4,
    dirs, slots, live, weights, inv_v, coup_v, diag_v, acc, cnt, sems, table_sems,
):
    subs, nblk, bs = diag.shape[0], diag.shape[1], diag.shape[2]
    own_slots = own.shape[0] // bs

    def loads(sub):
        pairs = ((coup, coup_v), (inv, inv_v), (diag, diag_v))
        return [
            pltpu.make_async_copy(a.at[sub], b.at[sub], sems.at[j, sub])
            for j, (a, b) in enumerate(pairs)
        ]

    for copy in loads(0):
        copy.start()
    tables = load_tables(
        (dirs_h, slots_h, live_h, weights_h), (dirs, slots, live, weights), table_sems
    )
    for sub in range(1, subs):
        for copy in loads(sub):
            copy.start()
    acc[...] = jnp.zeros_like(acc)
    cnt[...] = jnp.zeros_like(cnt)
    for copy in tables:
        copy.wait()

    def blocks(sub, count):
        c = coup_v[sub, :, :count * bs]
        st = jnp.dot(c.T, inv_v[sub], preferred_element_type=jnp.float32).astype(jnp.bfloat16)
        for k in range(count):
            cols = slice(k * bs, (k + 1) * bs)
            trail = jnp.dot(st[cols], c[:, cols], preferred_element_type=jnp.float32)
            block = (diag_v[sub, k].astype(jnp.float32) - trail).astype(jnp.bfloat16)
            schur[sub, k] = block
            w = weights[k, 0, sub].astype(jnp.float32)
            buf, slot = buffer_of(dirs[k, 0, sub]), slots[k, 0, sub]
            acc[buf * own_slots + slot] += w * block.astype(jnp.float32)
            cnt[buf, pl.ds(slot, 1), :] += jnp.full((1, bs), w, jnp.float32)

    def step(sub, carry):
        for copy in loads(sub):
            copy.wait()
        for count in range(1, nblk + 1):
            pl.when(live[0, sub] == count)(functools.partial(blocks, sub, count))
        return carry

    lax.fori_loop(0, subs, step, 0)
    for o in range(own_slots):
        own[o * bs:(o + 1) * bs] = acc[o]
    own_cnt[...] = cnt[0]
    for b, out in enumerate((s1, s2, s3, s4), 1):
        for o in range(own_slots):
            out[o * bs:(o + 1) * bs] = acc[b * own_slots + o].astype(jnp.bfloat16)
        out[own_slots * bs:] = cnt[b].astype(jnp.bfloat16)


def average_kernel(own, own_cnt, r1, r2, r3, r4, avg, avg_short):
    bs = own.shape[1]
    own_slots = own.shape[0] // bs
    parts = (r1, r2, r3, r4)
    count = own_cnt[...]
    for r in parts:
        count = count + r[own_slots * bs:].astype(jnp.float32)
    scale = 1.0 / jnp.maximum(count, 1.0)
    for o in range(own_slots):
        rows = slice(o * bs, (o + 1) * bs)
        total = own[rows]
        for r in parts:
            total = total + r[rows].astype(jnp.float32)
        mean = total * scale[o:o + 1]
        avg[rows] = mean
        avg_short[rows] = mean.astype(jnp.bfloat16)


def deviation_kernel(
    order, dirs_h, slots_h, live_h, schur, avg, r1, r2, r3, r4, dev,
    dirs, slots, live, table, stage, sems, table_sems,
):
    tables = load_tables((dirs_h, slots_h, live_h), (dirs, slots, live), table_sems)
    subs, nblk, bs = schur.shape[0], schur.shape[1], schur.shape[2]
    own_slots = avg.shape[0] // bs
    places = [0] + [1 + NAMES.index(name) for name in order]
    for b, r in zip(places, (avg, r1, r2, r3, r4)):
        for o in range(own_slots):
            table[b * own_slots + o] = r[o * bs:(o + 1) * bs]
    for copy in tables:
        copy.wait()
    stores = []
    for s in range(subs):
        for k in range(nblk):
            at = buffer_of(dirs[k, 0, s]) * own_slots + slots[k, 0, s]
            diff = schur[s, k].astype(jnp.float32) - table[at].astype(jnp.float32)
            stage[s, k] = jnp.where(k < live[0, s], diff, 0.0).astype(jnp.bfloat16)
        stores.append(pltpu.make_async_copy(stage.at[s], dev.at[s], sems.at[s]))
        stores[-1].start()
    for copy in stores:
        copy.wait()


def body(interior_inv, coupling, boundary_diag, directions, slot_ids, live_blocks, weights):
    inv, coup, diag = interior_inv[0, 0], coupling[0, 0], boundary_diag[0, 0]
    subs, ni, nb = coup.shape
    nblk, bs = diag.shape[1], diag.shape[2]
    own_slots = 8
    by_block = lambda x: jnp.transpose(x[0], (2, 0, 1))
    in_hbm = lambda x: pltpu.with_memory_space_constraint(x, pltpu.HBM)
    dirs, slots, wts = (in_hbm(by_block(x)) for x in (directions, slot_ids, weights))
    live = in_hbm(live_blocks[0])
    f32, bf16 = jnp.float32, jnp.bfloat16
    rows = own_slots * bs
    vmem = pl.BlockSpec(memory_space=pltpu.VMEM)
    hbm = pl.BlockSpec(memory_space=pltpu.HBM)
    schur, own, own_cnt, s1, s2, s3, s4 = pl.pallas_call(
        schur_kernel,
        in_specs=[hbm] * 7,
        out_specs=[vmem] * 7,
        out_shape=[
            pltpu.VMEM((subs, nblk, bs, bs), bf16),
            pltpu.VMEM((rows, bs), f32),
            pltpu.VMEM((PAD, bs), f32),
        ] + [pltpu.VMEM((rows + PAD, bs), bf16)] * 4,
        scratch_shapes=[
            pltpu.SMEM(dirs.shape, jnp.int32),
            pltpu.SMEM(slots.shape, jnp.int32),
            pltpu.SMEM(live.shape, jnp.int32),
            pltpu.SMEM(wts.shape, jnp.int32),
            pltpu.VMEM(inv.shape, bf16),
            pltpu.VMEM(coup.shape, bf16),
            pltpu.VMEM(diag.shape, bf16),
            pltpu.VMEM((5 * own_slots, bs, bs), f32),
            pltpu.VMEM((5, PAD, bs), f32),
            pltpu.SemaphoreType.DMA((3, subs)),
            pltpu.SemaphoreType.DMA((4,)),
        ],
        compiler_params=pltpu.CompilerParams(vmem_limit_bytes=56 * 2**20),
        name="schur_and_sums",
    )(dirs, slots, live, wts, in_hbm(inv), in_hbm(coup), in_hbm(diag))
    received = swap_all(dict(zip(NAMES, (s1, s2, s3, s4))), SUMS_ORDER)
    avg, avg_short = pl.pallas_call(
        average_kernel,
        in_specs=[vmem] * 6,
        out_specs=[vmem] * 2,
        out_shape=[
            jax.ShapeDtypeStruct((rows, bs), f32),
            jax.ShapeDtypeStruct((rows, bs), bf16),
        ],
        compiler_params=pltpu.CompilerParams(vmem_limit_bytes=16 * 2**20),
        name="average",
    )(own, own_cnt, *received)
    fetched = swap_all(dict.fromkeys(NAMES, avg_short), MEANS_ORDER)
    dev = pl.pallas_call(
        functools.partial(deviation_kernel, MEANS_ORDER),
        in_specs=[hbm] * 3 + [vmem] * 6,
        out_specs=hbm,
        out_shape=jax.ShapeDtypeStruct((subs, nblk, bs, bs), bf16),
        scratch_shapes=[
            pltpu.SMEM(dirs.shape, jnp.int32),
            pltpu.SMEM(slots.shape, jnp.int32),
            pltpu.SMEM(live.shape, jnp.int32),
            pltpu.VMEM((5 * own_slots, bs, bs), bf16),
            pltpu.VMEM((subs, nblk, bs, bs), bf16),
            pltpu.SemaphoreType.DMA((subs,)),
            pltpu.SemaphoreType.DMA((3,)),
        ],
        compiler_params=pltpu.CompilerParams(vmem_limit_bytes=16 * 2**20),
        name="deviation",
    )(dirs, slots, live, schur, avg_short, *fetched)
    return avg.reshape(1, 1, own_slots, bs, bs), dev[None, None]


def solution(mesh):
    return jax.shard_map(
        body,
        mesh=mesh,
        in_specs=(
            P("circ", "axial", None, None, None),
            P("circ", "axial", None, None, None),
            P("circ", "axial", None, None, None, None),
            P("circ", "axial", None, None),
            P("circ", "axial", None, None),
            P("circ", "axial", None),
            P("circ", "axial", None, None),
        ),
        out_specs=(
            P("circ", "axial", None, None, None),
            P("circ", "axial", None, None, None, None),
        ),
        check_vma=False,
    )
```

```python
import functools

import jax
import jax.numpy as jnp
from jax import lax
from jax.experimental import pallas as pl
from jax.experimental.pallas import tpu as pltpu
from jax.sharding import PartitionSpec as P

PAD = 16
SUMS_ORDER = ("near_a", "far_c", "far_a", "near_c")
MEANS_ORDER = ("far_a", "far_c", "near_c", "near_a")


def near_pairs(count):
    return [(i, i ^ 1) for i in range(count)]


def far_pairs(count, periodic):
    pairs = []
    for i in range(count):
        j = i + 1 if i % 2 else i - 1
        if periodic:
            pairs.append((i, j % count))
        elif 0 <= j < count:
            pairs.append((i, j))
    return pairs


NAMES = ("near_c", "far_c", "near_a", "far_a")


def swap_all(sent, order):
    circ, axial = lax.axis_size("circ"), lax.axis_size("axial")
    routes = {
        "near_c": ("circ", near_pairs(circ)),
        "far_c": ("circ", far_pairs(circ, True)),
        "near_a": ("axial", near_pairs(axial)),
        "far_a": ("axial", far_pairs(axial, False)),
    }
    diagonal = []
    for row in range(circ):
        for i, j in far_pairs(axial, False):
            diagonal.append((row * axial + i, row * axial + j))
        for i in (0, axial - 1):
            diagonal.append((row * axial + i, (row ^ 1) * axial + i))
    routes["far_a"] = (("circ", "axial"), diagonal)
    return [lax.ppermute(sent[name], *routes[name]) for name in order]


def buffer_of(code):
    odd_c = lax.rem(lax.axis_index("circ"), 2)
    odd_a = lax.rem(lax.axis_index("axial"), 2)
    circ = jnp.where(odd_c == 0, code, 3 - code)
    axial = jnp.where(odd_a == 0, code, 7 - code)
    return jnp.where(code == 0, 0, jnp.where(code <= 2, circ, axial))


def load_tables(sources, tables, sems):
    copies = [
        pltpu.make_async_copy(a, b, sems.at[j]) for j, (a, b) in enumerate(zip(sources, tables))
    ]
    for copy in copies:
        copy.start()
    return copies


def schur_kernel(
    dirs_h, slots_h, live_h, weights_h, inv, coup, diag,
    schur, own, own_cnt, s1, s2, s3, s4, places,
    dirs, slots, live, weights, inv_v, coup_v, diag_v, acc, cnt, sems, table_sems,
):
    subs, nblk, bs = diag.shape[0], diag.shape[1], diag.shape[2]
    own_slots = own.shape[0] // bs

    def loads(sub):
        pairs = ((coup, coup_v), (inv, inv_v), (diag, diag_v))
        return [
            pltpu.make_async_copy(a.at[sub], b.at[sub], sems.at[j, sub])
            for j, (a, b) in enumerate(pairs)
        ]

    for copy in loads(0):
        copy.start()
    tables = load_tables(
        (dirs_h, slots_h, live_h, weights_h), (dirs, slots, live, weights), table_sems
    )
    for sub in range(1, subs):
        for copy in loads(sub):
            copy.start()
    acc[...] = jnp.zeros_like(acc)
    cnt[...] = jnp.zeros_like(cnt)
    for copy in tables:
        copy.wait()

    def blocks(sub, count):
        c = coup_v[sub, :, :count * bs]
        st = jnp.dot(c.T, inv_v[sub], preferred_element_type=jnp.float32).astype(jnp.bfloat16)
        for k in range(count):
            cols = slice(k * bs, (k + 1) * bs)
            trail = jnp.dot(st[cols], c[:, cols], preferred_element_type=jnp.float32)
            block = (diag_v[sub, k].astype(jnp.float32) - trail).astype(jnp.bfloat16)
            schur[sub, k] = block
            w = weights[k, 0, sub].astype(jnp.float32)
            buf, slot = buffer_of(dirs[k, 0, sub]), slots[k, 0, sub]
            acc[buf * own_slots + slot] += w * block.astype(jnp.float32)
            cnt[buf, pl.ds(slot, 1), :] += jnp.full((1, bs), w, jnp.float32)

    def step(sub, carry):
        for copy in loads(sub):
            copy.wait()
        for count in range(1, nblk + 1):
            pl.when(live[0, sub] == count)(functools.partial(blocks, sub, count))
        return carry

    for sub in range(subs):
        for k in range(nblk):
            at = buffer_of(dirs[k, 0, sub]) * own_slots + slots[k, 0, sub]
            places[k, sub] = jnp.where(k < live[0, sub], at, -1)
    lax.fori_loop(0, subs, step, 0)
    for o in range(own_slots):
        own[o * bs:(o + 1) * bs] = acc[o]
    own_cnt[...] = cnt[0]
    for b, out in enumerate((s1, s2, s3, s4), 1):
        for o in range(own_slots):
            out[o * bs:(o + 1) * bs] = acc[b * own_slots + o].astype(jnp.bfloat16)
        out[own_slots * bs:] = cnt[b].astype(jnp.bfloat16)


def average_kernel(own, own_cnt, r1, r2, r3, r4, avg, avg_short):
    bs = own.shape[1]
    own_slots = own.shape[0] // bs
    parts = (r1, r2, r3, r4)
    count = own_cnt[...]
    for r in parts:
        count = count + r[own_slots * bs:].astype(jnp.float32)
    scale = 1.0 / jnp.maximum(count, 1.0)
    for o in range(own_slots):
        rows = slice(o * bs, (o + 1) * bs)
        total = own[rows]
        for r in parts:
            total = total + r[rows].astype(jnp.float32)
        mean = total * scale[o:o + 1]
        avg[rows] = mean
        avg_short[rows] = mean.astype(jnp.bfloat16)


def deviation_kernel(
    order, at, schur, mean, avg, r1, r2, r3, r4, mean_out, dev, table, stage, sems, mean_sem
):
    mean_copy = pltpu.make_async_copy(mean, mean_out, mean_sem)
    mean_copy.start()
    subs, nblk, bs = schur.shape[0], schur.shape[1], schur.shape[2]
    own_slots = avg.shape[0] // bs
    segments = [0] + [1 + NAMES.index(name) for name in order]
    for b, r in zip(segments, (avg, r1, r2, r3, r4)):
        for o in range(own_slots):
            table[b * own_slots + o] = r[o * bs:(o + 1) * bs]
    stores = []
    for s in range(subs):
        for k in range(nblk):
            place = at[k, s]
            diff = schur[s, k] - table[jnp.maximum(place, 0)]
            stage[s, k] = jnp.where(place >= 0, diff, jnp.zeros_like(diff))
        stores.append(pltpu.make_async_copy(stage.at[s], dev.at[s], sems.at[s]))
        stores[-1].start()
    for copy in stores:
        copy.wait()
    mean_copy.wait()


def body(interior_inv, coupling, boundary_diag, directions, slot_ids, live_blocks, weights):
    inv, coup, diag = interior_inv[0, 0], coupling[0, 0], boundary_diag[0, 0]
    subs, ni, nb = coup.shape
    nblk, bs = diag.shape[1], diag.shape[2]
    own_slots = 8
    by_block = lambda x: jnp.transpose(x[0], (2, 0, 1))
    in_hbm = lambda x: pltpu.with_memory_space_constraint(x, pltpu.HBM)
    dirs, slots, wts = (in_hbm(by_block(x)) for x in (directions, slot_ids, weights))
    live = in_hbm(live_blocks[0])
    f32, bf16 = jnp.float32, jnp.bfloat16
    rows = own_slots * bs
    vmem = pl.BlockSpec(memory_space=pltpu.VMEM)
    hbm = pl.BlockSpec(memory_space=pltpu.HBM)
    smem = pl.BlockSpec(memory_space=pltpu.SMEM)
    schur, own, own_cnt, s1, s2, s3, s4, places = pl.pallas_call(
        schur_kernel,
        in_specs=[hbm] * 7,
        out_specs=[vmem] * 7 + [smem],
        out_shape=[
            pltpu.VMEM((subs, nblk, bs, bs), bf16),
            pltpu.VMEM((rows, bs), f32),
            pltpu.VMEM((PAD, bs), f32),
        ] + [pltpu.VMEM((rows + PAD, bs), bf16)] * 4 + [pltpu.SMEM((nblk, subs), jnp.int32)],
        scratch_shapes=[
            pltpu.SMEM(dirs.shape, jnp.int32),
            pltpu.SMEM(slots.shape, jnp.int32),
            pltpu.SMEM(live.shape, jnp.int32),
            pltpu.SMEM(wts.shape, jnp.int32),
            pltpu.VMEM(inv.shape, bf16),
            pltpu.VMEM(coup.shape, bf16),
            pltpu.VMEM(diag.shape, bf16),
            pltpu.VMEM((5 * own_slots, bs, bs), f32),
            pltpu.VMEM((5, PAD, bs), f32),
            pltpu.SemaphoreType.DMA((3, subs)),
            pltpu.SemaphoreType.DMA((4,)),
        ],
        compiler_params=pltpu.CompilerParams(vmem_limit_bytes=56 * 2**20),
        name="schur_and_sums",
    )(dirs, slots, live, wts, in_hbm(inv), in_hbm(coup), in_hbm(diag))
    received = swap_all(dict(zip(NAMES, (s1, s2, s3, s4))), SUMS_ORDER)
    avg, avg_short = pl.pallas_call(
        average_kernel,
        in_specs=[vmem] * 6,
        out_specs=[vmem] * 2,
        out_shape=[
            pltpu.VMEM((rows, bs), f32),
            pltpu.VMEM((rows, bs), bf16),
        ],
        compiler_params=pltpu.CompilerParams(vmem_limit_bytes=16 * 2**20),
        name="average",
    )(own, own_cnt, *received)
    fetched = swap_all(dict.fromkeys(NAMES, avg_short), MEANS_ORDER)
    averaged, dev = pl.pallas_call(
        functools.partial(deviation_kernel, MEANS_ORDER),
        in_specs=[smem] + [vmem] * 7,
        out_specs=[hbm] * 2,
        out_shape=[
            jax.ShapeDtypeStruct((rows, bs), f32),
            jax.ShapeDtypeStruct((subs, nblk, bs, bs), bf16),
        ],
        scratch_shapes=[
            pltpu.VMEM((5 * own_slots, bs, bs), bf16),
            pltpu.VMEM((subs, nblk, bs, bs), bf16),
            pltpu.SemaphoreType.DMA((subs,)),
            pltpu.SemaphoreType.DMA,
        ],
        compiler_params=pltpu.CompilerParams(vmem_limit_bytes=16 * 2**20),
        name="deviation",
    )(pltpu.with_memory_space_constraint(places, pltpu.SMEM), schur, avg, avg_short, *fetched)
    return averaged.reshape(1, 1, own_slots, bs, bs), dev[None, None]


def solution(mesh):
    return jax.shard_map(
        body,
        mesh=mesh,
        in_specs=(
            P("circ", "axial", None, None, None),
            P("circ", "axial", None, None, None),
            P("circ", "axial", None, None, None, None),
            P("circ", "axial", None, None),
            P("circ", "axial", None, None),
            P("circ", "axial", None),
            P("circ", "axial", None, None),
        ),
        out_specs=(
            P("circ", "axial", None, None, None),
            P("circ", "axial", None, None, None, None),
        ),
        check_vma=False,
    )
```

```python
import functools

import jax
import jax.numpy as jnp
from jax import lax
from jax.experimental import pallas as pl
from jax.experimental.pallas import tpu as pltpu
from jax.sharding import PartitionSpec as P

PAD = 16
SUMS_ORDER = ("axial_1", "far_c", "axial_2", "near_c")
FIRST_ROWS = 2
MEANS_ORDER = ("axial_2", "far_c", "near_c", "axial_1")


def near_pairs(count):
    return [(i, i ^ 1) for i in range(count)]


def far_pairs(count, periodic):
    pairs = []
    for i in range(count):
        j = i + 1 if i % 2 else i - 1
        if periodic:
            pairs.append((i, j % count))
        elif 0 <= j < count:
            pairs.append((i, j))
    return pairs


NAMES = ("near_c", "far_c", "axial_1", "axial_2")


def near_first(row):
    return row < FIRST_ROWS


def swap_all(sent, order):
    circ, axial = lax.axis_size("circ"), lax.axis_size("axial")
    first, second = [], []
    for row in range(circ):
        at = lambda i, row=row: row * axial + i
        close = [(at(i), at(j)) for i, j in near_pairs(axial)]
        across = [(at(i), at(j)) for i, j in far_pairs(axial, False)]
        across += [(at(i), (row ^ 1) * axial + i) for i in (0, axial - 1)]
        first += close if near_first(row) else across
        second += across if near_first(row) else close
    routes = {
        "near_c": ("circ", near_pairs(circ)),
        "far_c": ("circ", far_pairs(circ, True)),
        "axial_1": (("circ", "axial"), first),
        "axial_2": (("circ", "axial"), second),
    }
    return [lax.ppermute(sent[name], *routes[name]) for name in order]


def buffer_of(code):
    odd_c = lax.rem(lax.axis_index("circ"), 2) == 1
    odd_a = lax.rem(lax.axis_index("axial"), 2) == 1
    circ = jnp.where(odd_c, 3 - code, code)
    is_near = (code == 3) != odd_a
    axial = jnp.where(is_near == near_first(lax.axis_index("circ")), 3, 4)
    return jnp.where(code == 0, 0, jnp.where(code <= 2, circ, axial))


def load_tables(sources, tables, sems):
    copies = [
        pltpu.make_async_copy(a, b, sems.at[j]) for j, (a, b) in enumerate(zip(sources, tables))
    ]
    for copy in copies:
        copy.start()
    return copies


def schur_kernel(
    dirs_h, slots_h, live_h, weights_h, inv, coup, diag,
    schur, own, own_cnt, s1, s2, s3, s4, places,
    dirs, slots, live, weights, inv_v, coup_v, diag_v, acc, cnt, sems, table_sems,
):
    subs, nblk, bs = diag.shape[0], diag.shape[1], diag.shape[2]
    own_slots = own.shape[0] // bs

    def loads(sub):
        pairs = ((coup, coup_v), (inv, inv_v), (diag, diag_v))
        return [
            pltpu.make_async_copy(a.at[sub], b.at[sub], sems.at[j, sub])
            for j, (a, b) in enumerate(pairs)
        ]

    for copy in loads(0):
        copy.start()
    tables = load_tables(
        (dirs_h, slots_h, live_h, weights_h), (dirs, slots, live, weights), table_sems
    )
    for sub in range(1, subs):
        for copy in loads(sub):
            copy.start()
    acc[...] = jnp.zeros_like(acc)
    cnt[...] = jnp.zeros_like(cnt)
    for copy in tables:
        copy.wait()

    def blocks(sub, count):
        c = coup_v[sub, :, :count * bs]
        st = jnp.dot(c.T, inv_v[sub], preferred_element_type=jnp.float32).astype(jnp.bfloat16)
        for k in range(count):
            cols = slice(k * bs, (k + 1) * bs)
            trail = jnp.dot(st[cols], c[:, cols], preferred_element_type=jnp.float32)
            block = (diag_v[sub, k].astype(jnp.float32) - trail).astype(jnp.bfloat16)
            schur[sub, k] = block
            w = weights[k, 0, sub].astype(jnp.float32)
            buf, slot = buffer_of(dirs[k, 0, sub]), slots[k, 0, sub]
            acc[buf * own_slots + slot] += w * block.astype(jnp.float32)
            cnt[buf, pl.ds(slot, 1), :] += jnp.full((1, bs), w, jnp.float32)

    def step(sub, carry):
        for copy in loads(sub):
            copy.wait()
        for count in range(1, nblk + 1):
            pl.when(live[0, sub] == count)(functools.partial(blocks, sub, count))
        return carry

    for sub in range(subs):
        for k in range(nblk):
            at = buffer_of(dirs[k, 0, sub]) * own_slots + slots[k, 0, sub]
            places[k, sub] = jnp.where(k < live[0, sub], at, -1)
    lax.fori_loop(0, subs, step, 0)
    for o in range(own_slots):
        own[o * bs:(o + 1) * bs] = acc[o]
    own_cnt[...] = cnt[0]
    for b, out in enumerate((s1, s2, s3, s4), 1):
        for o in range(own_slots):
            out[o * bs:(o + 1) * bs] = acc[b * own_slots + o].astype(jnp.bfloat16)
        out[own_slots * bs:] = cnt[b].astype(jnp.bfloat16)


def average_kernel(own, own_cnt, r1, r2, r3, r4, avg, avg_short):
    bs = own.shape[1]
    own_slots = own.shape[0] // bs
    parts = (r1, r2, r3, r4)
    count = own_cnt[...]
    for r in parts:
        count = count + r[own_slots * bs:].astype(jnp.float32)
    scale = 1.0 / jnp.maximum(count, 1.0)
    for o in range(own_slots):
        rows = slice(o * bs, (o + 1) * bs)
        total = own[rows]
        for r in parts:
            total = total + r[rows].astype(jnp.float32)
        mean = total * scale[o:o + 1]
        avg[rows] = mean
        avg_short[rows] = mean.astype(jnp.bfloat16)


def deviation_kernel(
    order, at, schur, mean, avg, r1, r2, r3, r4, mean_out, dev, table, stage, sems, mean_sem
):
    mean_copy = pltpu.make_async_copy(mean, mean_out, mean_sem)
    mean_copy.start()
    subs, nblk, bs = schur.shape[0], schur.shape[1], schur.shape[2]
    own_slots = avg.shape[0] // bs
    segments = [0] + [1 + NAMES.index(name) for name in order]
    for b, r in zip(segments, (avg, r1, r2, r3, r4)):
        for o in range(own_slots):
            table[b * own_slots + o] = r[o * bs:(o + 1) * bs]
    stores = []
    for s in range(subs):
        for k in range(nblk):
            place = at[k, s]
            diff = schur[s, k] - table[jnp.maximum(place, 0)]
            stage[s, k] = jnp.where(place >= 0, diff, jnp.zeros_like(diff))
        stores.append(pltpu.make_async_copy(stage.at[s], dev.at[s], sems.at[s]))
        stores[-1].start()
    for copy in stores:
        copy.wait()
    mean_copy.wait()


def body(interior_inv, coupling, boundary_diag, directions, slot_ids, live_blocks, weights):
    inv, coup, diag = interior_inv[0, 0], coupling[0, 0], boundary_diag[0, 0]
    subs, ni, nb = coup.shape
    nblk, bs = diag.shape[1], diag.shape[2]
    own_slots = 8
    by_block = lambda x: jnp.transpose(x[0], (2, 0, 1))
    in_hbm = lambda x: pltpu.with_memory_space_constraint(x, pltpu.HBM)
    dirs, slots, wts = (in_hbm(by_block(x)) for x in (directions, slot_ids, weights))
    live = in_hbm(live_blocks[0])
    f32, bf16 = jnp.float32, jnp.bfloat16
    rows = own_slots * bs
    vmem = pl.BlockSpec(memory_space=pltpu.VMEM)
    hbm = pl.BlockSpec(memory_space=pltpu.HBM)
    smem = pl.BlockSpec(memory_space=pltpu.SMEM)
    schur, own, own_cnt, s1, s2, s3, s4, places = pl.pallas_call(
        schur_kernel,
        in_specs=[hbm] * 7,
        out_specs=[vmem] * 7 + [smem],
        out_shape=[
            pltpu.VMEM((subs, nblk, bs, bs), bf16),
            pltpu.VMEM((rows, bs), f32),
            pltpu.VMEM((PAD, bs), f32),
        ] + [pltpu.VMEM((rows + PAD, bs), bf16)] * 4 + [pltpu.SMEM((nblk, subs), jnp.int32)],
        scratch_shapes=[
            pltpu.SMEM(dirs.shape, jnp.int32),
            pltpu.SMEM(slots.shape, jnp.int32),
            pltpu.SMEM(live.shape, jnp.int32),
            pltpu.SMEM(wts.shape, jnp.int32),
            pltpu.VMEM(inv.shape, bf16),
            pltpu.VMEM(coup.shape, bf16),
            pltpu.VMEM(diag.shape, bf16),
            pltpu.VMEM((5 * own_slots, bs, bs), f32),
            pltpu.VMEM((5, PAD, bs), f32),
            pltpu.SemaphoreType.DMA((3, subs)),
            pltpu.SemaphoreType.DMA((4,)),
        ],
        compiler_params=pltpu.CompilerParams(vmem_limit_bytes=56 * 2**20),
        name="schur_and_sums",
    )(dirs, slots, live, wts, in_hbm(inv), in_hbm(coup), in_hbm(diag))
    received = swap_all(dict(zip(NAMES, (s1, s2, s3, s4))), SUMS_ORDER)
    avg, avg_short = pl.pallas_call(
        average_kernel,
        in_specs=[vmem] * 6,
        out_specs=[vmem] * 2,
        out_shape=[
            pltpu.VMEM((rows, bs), f32),
            pltpu.VMEM((rows, bs), bf16),
        ],
        compiler_params=pltpu.CompilerParams(vmem_limit_bytes=16 * 2**20),
        name="average",
    )(own, own_cnt, *received)
    fetched = swap_all(dict.fromkeys(NAMES, avg_short), MEANS_ORDER)
    averaged, dev = pl.pallas_call(
        functools.partial(deviation_kernel, MEANS_ORDER),
        in_specs=[smem] + [vmem] * 7,
        out_specs=[hbm] * 2,
        out_shape=[
            jax.ShapeDtypeStruct((rows, bs), f32),
            jax.ShapeDtypeStruct((subs, nblk, bs, bs), bf16),
        ],
        scratch_shapes=[
            pltpu.VMEM((5 * own_slots, bs, bs), bf16),
            pltpu.VMEM((subs, nblk, bs, bs), bf16),
            pltpu.SemaphoreType.DMA((subs,)),
            pltpu.SemaphoreType.DMA,
        ],
        compiler_params=pltpu.CompilerParams(vmem_limit_bytes=16 * 2**20),
        name="deviation",
    )(pltpu.with_memory_space_constraint(places, pltpu.SMEM), schur, avg, avg_short, *fetched)
    return averaged.reshape(1, 1, own_slots, bs, bs), dev[None, None]


def solution(mesh):
    return jax.shard_map(
        body,
        mesh=mesh,
        in_specs=(
            P("circ", "axial", None, None, None),
            P("circ", "axial", None, None, None),
            P("circ", "axial", None, None, None, None),
            P("circ", "axial", None, None),
            P("circ", "axial", None, None),
            P("circ", "axial", None),
            P("circ", "axial", None, None),
        ),
        out_specs=(
            P("circ", "axial", None, None, None),
            P("circ", "axial", None, None, None, None),
        ),
        check_vma=False,
    )
```
